32 devices in a mesh: row: 4 (over y, x), col: 8 (over z, core).
Axes of the slice: x: 2, y: 2, z: 4, core: 2. Of those that a mesh axis runs over, the one named last changes fastest.
Arguments:
- positions: float32 [3, 4096], P(None, ('row', 'col')), may hold values from 0 to 5
- species: int32 [4096], P(('row', 'col')), may hold values from 0 to 99
- tile_list: int32 [4, 8, 2, 3], P('row', 'col'), may hold values from 0 to 7, as said below
- pair_mask: int32 [4, 8, 2, 128, 128], P('row', 'col'), may hold values 0 or 1
- embed: float32 [100, 128], replicated, may hold values from -6 to 6
- w_in: float32 [2, 128, 128], replicated, may hold values from -0.5 to 0.5
- rbf_weight: bfloat16 [2, 256, 128], replicated, may hold values from -1 to 1
- rbf_bias: float32 [2, 128], replicated, may hold values from -4 to 4
- filt_weight: bfloat16 [2, 128, 128], replicated, may hold values from -1 to 1
- w_update1: float32 [2, 128, 128], replicated, may hold values from -1 to 1
- w_update2: float32 [2, 128, 128], replicated, may hold values from -0.5 to 0.5
- w_out1: float32 [128, 64], replicated, may hold values from -0.5 to 0.5
- w_out2: float32 [64], replicated, may hold values from -0.75 to 0.75
Outputs:
- atom_energy: float32 [4096], P(('row', 'col'))
- forces: float32 [3, 4096], P(None, ('row', 'col'))
The draws below stay inside these ranges and needn't reach their ends.
Inputs may be any that keep to these rules, and one draw needn't show every extreme that they name: `tile_list`: A live slot (flag 1) names a row block below 8 and a column block below 4; the live slots of one device name distinct row blocks and come first; a dead slot is all zeros; every device has at least one live slot and some device has all 2.
All inputs are finite; a program needn't handle non-finite values. No bound on the sum of `pair_mask` on one device may be relied on, other than what follows from the above.
Results may differ from the reference program's by a relative error of at most 0.007.
Values sent between devices are 32-bit elements; how exact they have to be, the bound alone decides.
A program may use at most 192 MiB of HBM per device.

```python
import math
import jax
import jax.numpy as jnp
from jax import lax

BLK = 128
FILTERS = 128
GAUSS = 256
SPECIES = 100
HALF = 64
LAYERS = 2
KMAX = 2
NATOM = 4096
N_ROW = 4
N_COL = 8


def draw_tile_list(key, part):
    key_order, key_col, key_count, key_pick = jax.random.split(key, 4)
    devices_all = N_ROW * N_COL
    scores = jax.random.randint(key_order, (devices_all, N_COL), 0, 1 << 20) * N_COL + jnp.arange(N_COL, dtype=jnp.int32)[None, :]
    order = jnp.argsort(scores, axis=1)[:, :KMAX].astype(jnp.int32)
    col_pick = jax.random.randint(key_col, (devices_all, KMAX), 0, N_ROW).astype(jnp.int32)
    counts = jax.random.randint(key_count, (devices_all,), 1, KMAX + 1).astype(jnp.int32)
    chosen = jax.random.randint(key_pick, (), 0, devices_all)
    counts = jnp.where(jnp.arange(devices_all, dtype=jnp.int32) == chosen, KMAX, counts)
    live = (jnp.arange(KMAX, dtype=jnp.int32)[None, :] < counts[:, None]).astype(jnp.int32)
    table = jnp.stack([order * live, col_pick * live, live], axis=-1)
    return table.reshape(N_ROW, N_COL, KMAX, 3)


def plant(result, key, smallest, high):
    dims = result.shape
    place = [jax.random.randint(jax.random.fold_in(key, axis), (), 0, dims[axis]) for axis in range(len(dims))]
    result = result.at[tuple(place)].set(smallest)
    longest = dims.index(max(dims))
    place[longest] = (place[longest] + 1) % dims[longest]
    return result.at[tuple(place)].set(high)


def steps_of(stream_key, dims, shards, least, high):
    gain = 1.0
    for axis_at, shards_of in shards:
        draws = jax.random.uniform(jax.random.fold_in(jax.random.fold_in(stream_key, 6), axis_at), (shards_of,), jnp.float32, least / len(shards), high / len(shards))
        gain = gain * jnp.repeat(jnp.exp(draws), dims[axis_at] // shards_of).reshape((-1,) + (1,) * (len(dims) - 1 - axis_at))
    return gain


def scatter_about(key, dims, width, most, kind=jnp.bfloat16):
    values = jax.random.normal(key, dims, jnp.float32) * width
    return jnp.minimum(jnp.maximum(values, -most), most).astype(kind)


def setup_inputs(seed: int = 0) -> dict:
    key_list = jax.random.split(jax.random.key(seed), 14)
    positions = jnp.clip(5.0 * jax.random.uniform(key_list[0], (3, NATOM), jnp.float32) ** steps_of(key_list[0], (3, NATOM), ((1, 32),), -0.2, 0.2), 0.0, 5.0)
    species = plant(jax.random.randint(key_list[1], (NATOM,), 0, SPECIES), jax.random.fold_in(key_list[1], 1), 0, SPECIES - 1).astype(jnp.int32)
    tile_list = draw_tile_list(jax.random.fold_in(key_list[13], 71), 0)
    pair_mask = plant((jax.random.randint(key_list[3], (N_ROW, N_COL, KMAX, BLK, BLK), 0, 2) < 1).astype(jnp.int32), jax.random.fold_in(key_list[3], 1), 0, 1)
    embed = scatter_about(key_list[4], (SPECIES, FILTERS), 1.0, 6.0, jnp.float32)
    w_in = scatter_about(key_list[5], (LAYERS, FILTERS, FILTERS), FILTERS ** -0.5, 0.5, jnp.float32)
    rbf_weight = scatter_about(key_list[6], (LAYERS, GAUSS, FILTERS), (GAUSS // 8) ** -0.5, 1.0)
    rbf_bias = scatter_about(key_list[7], (LAYERS, FILTERS), 0.7, 4.0, jnp.float32)
    filt_weight = scatter_about(key_list[8], (LAYERS, FILTERS, FILTERS), (FILTERS // 4) ** -0.5, 1.0)
    w_update1 = scatter_about(key_list[9], (LAYERS, FILTERS, FILTERS), (FILTERS // 4) ** -0.5, 1.0, jnp.float32)
    w_update2 = scatter_about(key_list[10], (LAYERS, FILTERS, FILTERS), FILTERS ** -0.5, 0.5, jnp.float32)
    w_out1 = scatter_about(key_list[11], (FILTERS, HALF), FILTERS ** -0.5, 0.5, jnp.float32)
    w_out2 = scatter_about(key_list[12], (HALF,), HALF ** -0.5, 0.75, jnp.float32)
    return {"positions": positions, "species": species, "tile_list": tile_list, "pair_mask": pair_mask, "embed": embed, "w_in": w_in, "rbf_weight": rbf_weight, "rbf_bias": rbf_bias, "filt_weight": filt_weight, "w_update1": w_update1, "w_update2": w_update2, "w_out1": w_out1, "w_out2": w_out2}


CUTOFF = 5.0
NORM_DIV = 4.0
HIGH = lax.Precision.HIGHEST

def shifted_softplus(values):
    return jax.nn.softplus(values) - math.log(2.0)

def tile_message(row_coord, col_coord, col_feat, pair_gate, rbf_w, rbf_b, filt_w):
    offset = row_coord[:, :, None] - col_coord[:, None, :]
    distance = jnp.sqrt(lax.optimization_barrier(jnp.sum(offset * offset, axis=0)) + 0.01)
    n_gauss = rbf_w.shape[0]
    rows_here = distance.shape[0]
    feat_width = filt_w.shape[1]
    centers = jnp.arange(n_gauss).astype(distance.dtype) * (CUTOFF / n_gauss)
    sharpness = (n_gauss / CUTOFF) ** 2 / 32.0
    expand = jnp.exp(-sharpness * (distance[:, :, None] - centers) ** 2).astype(jnp.bfloat16)
    pre_act = jnp.dot(expand.reshape(rows_here * rows_here, n_gauss), rbf_w, preferred_element_type=jnp.float32) + rbf_b
    hidden = shifted_softplus(pre_act).astype(jnp.bfloat16)
    filters = jnp.dot(hidden, filt_w, preferred_element_type=jnp.float32).reshape(rows_here, rows_here, feat_width)
    envelope = jnp.where(distance < CUTOFF, 0.5 * (jnp.cos(math.pi * distance / CUTOFF) + 1.0), 0.0)
    envelope = envelope * pair_gate.astype(distance.dtype)
    return jnp.einsum('ijf,ij,jf->if', filters, envelope, col_feat) / NORM_DIV

def atom_update(message, w_one, w_two):
    return jnp.dot(shifted_softplus(jnp.dot(message, w_one, precision=HIGH)), w_two, precision=HIGH)

def energy_head(features, w_out1, w_out2):
    return jnp.dot(shifted_softplus(jnp.dot(features, w_out1, precision=HIGH)), w_out2, precision=HIGH)

def energy_parts(positions, species, tile_list, pair_mask, embed, w_in, rbf_weight, rbf_bias, filt_weight, w_update1, w_update2, w_out1, w_out2):
    n_blocks = N_ROW * N_COL
    onehot = (species[:, None] == jnp.arange(SPECIES, dtype=jnp.int32)[None, :]).astype(embed.dtype)
    features = jnp.dot(onehot, embed, precision=HIGH)
    table = tile_list.reshape(N_ROW * N_COL * KMAX, 3)
    flat_idx = jnp.arange(N_ROW * N_COL * KMAX, dtype=jnp.int32)
    row_dev = flat_idx // (N_COL * KMAX)
    col_dev = flat_idx // KMAX % N_COL
    row_block = row_dev * N_COL + table[:, 0]
    col_block = table[:, 1] * N_COL + col_dev
    gates = pair_mask.reshape(N_ROW * N_COL * KMAX, BLK, BLK) * table[:, 2][:, None, None]
    block_pos = jnp.transpose(positions.reshape(3, n_blocks, BLK), (1, 0, 2))
    row_coord = block_pos[row_block]
    col_coord = block_pos[col_block]
    for layer_idx in range(LAYERS):
        mixed_in = jnp.dot(features, w_in[layer_idx], precision=HIGH)
        block_feat = mixed_in.reshape(n_blocks, BLK, FILTERS)
        rbf_w = rbf_weight[layer_idx]
        rbf_b = rbf_bias[layer_idx]
        filt_w = filt_weight[layer_idx]

        def one_tile(operands, rbf_w=rbf_w, rbf_b=rbf_b, filt_w=filt_w):
            return tile_message(operands[0], operands[1], operands[2], operands[3], rbf_w, rbf_b, filt_w)
        msgs = lax.map(jax.checkpoint(one_tile), (row_coord, col_coord, block_feat[col_block], gates))
        message = jnp.zeros((n_blocks, BLK, FILTERS), features.dtype).at[row_block].add(msgs)
        message = message.reshape(n_blocks * BLK, FILTERS)
        features = features + atom_update(message, w_update1[layer_idx], w_update2[layer_idx])
    return energy_head(features, w_out1, w_out2)

def reference(positions, species, tile_list, pair_mask, embed, w_in, rbf_weight, rbf_bias, filt_weight, w_update1, w_update2, w_out1, w_out2):

    def total_fn(coords):
        return energy_parts(coords, species, tile_list, pair_mask, embed, w_in, rbf_weight, rbf_bias, filt_weight, w_update1, w_update2, w_out1, w_out2)
    energies, pull_back = jax.vjp(total_fn, positions)
    grads = pull_back(jnp.ones_like(energies))[0]
    return (energies, -grads)
```

```python
from functools import partial
import math

import jax
import jax.numpy as jnp
from jax import lax
from jax.experimental import pallas as pl
from jax.experimental.pallas import tpu as pltpu
from jax.sharding import PartitionSpec as P

CUTOFF = 5.0
NORM_DIV = 4.0
HIGH = lax.Precision.HIGHEST
MESH = pl.DeviceIdType.MESH
GROUP = 8
SUB = 4
F32 = jnp.float32
BF16 = jnp.bfloat16


def ssp_parts(values):
    th = jnp.tanh(0.5 * values)
    return jnp.maximum(values, 0.0) - jnp.log(1.0 + jnp.abs(th)), 0.5 * (1.0 + th)


def dot_nn(a, b):
    return lax.dot_general(a, b, (((1,), (0,)), ((), ())), precision=HIGH, preferred_element_type=F32)


def dot_nt(a, b):
    return lax.dot_general(a, b, (((1,), (1,)), ((), ())), precision=HIGH, preferred_element_type=F32)


def kernel(
    n_row, n_col, slots,
    tl, pos, spec, mask, embed, w_in, rbf_w, rbf_b, filt_w, wu1, wu2, wo1, wo2,
    e_out, f_out,
    posblk, rowpos, colpos, emb_s, wc, fc,
    ubuf, envb, envp, unit, es, ds, hs, ts,
    g1_s, dg_s, msg, sibmsg, sbuf, rbuf, xbuf0, xbuf1, gbuf0, gbuf1, dxs, dxsend, dxrecv,
    st, rfsend, rfrecv, cfsend, cfrecv,
    send_sem, recv_sem,
):
    blk = pos.shape[1]
    feat = w_in.shape[2]
    n_gauss = rbf_w.shape[1]
    nz = n_col // 2
    me_r = lax.axis_index("row")
    me_c = lax.axis_index("col")
    z = me_c // 2
    core = me_c % 2
    sib = z * 2 + (1 - core)
    started = []
    xbuf, gbuf = (xbuf0, xbuf1), (gbuf0, gbuf1)

    def send(src, dst, r, c):
        n = len(started)
        copy = pltpu.make_async_remote_copy(
            src_ref=src, dst_ref=dst, send_sem=send_sem.at[n], recv_sem=recv_sem.at[n],
            device_id=(r, c), device_id_type=MESH)
        copy.start()
        started.append(copy)
        return copy

    row_peers = [(lax.rem(me_r + o, n_row), me_c) for o in range(1, n_row)]
    col_peers = [(me_r, lax.rem(me_c + o, n_col)) for o in range(1, n_col)]
    same_peers = [lax.rem(z + o, nz) for o in range(1, nz)]

    barrier = pltpu.get_barrier_semaphore()
    for peer in row_peers + col_peers:
        pl.semaphore_signal(barrier, inc=1, device_id=peer, device_id_type=MESH)

    posblk[...] = jnp.zeros_like(posblk)
    posblk[0:3, :] = pos[...]
    for k in range(slots):
        posblk[3 + k:4 + k, :] = jnp.full((1, blk), tl[0, 0, k, 0], jnp.int32).astype(F32)
        posblk[3 + slots + k:4 + slots + k, :] = jnp.full((1, blk), tl[0, 0, k, 1], jnp.int32).astype(F32)
    rowpos[me_c] = posblk[...]
    colpos[me_r] = posblk[...]

    pl.semaphore_wait(barrier, len(row_peers) + len(col_peers))
    pos_copies = [send(posblk, rowpos.at[me_c], *peer) for peer in col_peers]
    pos_copies += [send(posblk, colpos.at[me_r], *peer) for peer in row_peers]

    emb_s[...] = jnp.zeros_like(emb_s)
    emb_s[0:embed.shape[0], :] = embed[...]
    onehot_t = (lax.broadcasted_iota(jnp.int32, (blk, blk), 0) == spec[...]).astype(F32)
    features = dot_nn(onehot_t.T, emb_s[...])

    def gather_features(layer, value):
        xbuf[layer][me_r] = value
        return [send(xbuf[layer].at[me_r], xbuf[layer].at[me_r], *peer) for peer in row_peers]

    x_copies = gather_features(0, dot_nn(features, w_in[0]))

    wc[:, 0:feat] = (rbf_w[0].astype(F32) * 0.5).astype(BF16)
    wc[:, feat:2 * feat] = (rbf_w[1].astype(F32) * 0.5).astype(BF16)
    fc[...] = jnp.zeros_like(fc)
    fc[0:feat, 0:feat] = (filt_w[0].astype(F32) * 2.0).astype(BF16)
    fc[feat:2 * feat, feat:2 * feat] = (filt_w[1].astype(F32) * 2.0).astype(BF16)
    bias = 0.5 * jnp.concatenate([rbf_b[0:1, :], rbf_b[1:2, :]], axis=1)

    sharp = (n_gauss / CUTOFF) ** 2 / 32.0
    alpha = math.sqrt(sharp / math.log(2.0))
    centers = lax.broadcasted_iota(jnp.int32, (1, n_gauss), 1).astype(F32) * (alpha * CUTOFF / n_gauss)
    half_kappa = -math.log(2.0) * alpha

    for copy in pos_copies:
        copy.wait_recv()

    rows = [tl[0, 0, k, 0] for k in range(slots)]
    cols = [tl[0, 0, k, 1] for k in range(slots)]
    for k in range(slots):
        rp = rowpos[rows[k]]
        cp = colpos[cols[k]]
        diffs = []
        for a in range(3):
            pj = jnp.broadcast_to(cp[a:a + 1, :], (blk, blk)).T
            diffs.append(rp[a:a + 1, :] - pj)
        dist = jnp.sqrt(diffs[0] * diffs[0] + diffs[1] * diffs[1] + diffs[2] * diffs[2] + 0.01)
        inv = 1.0 / dist
        for a in range(3):
            unit[k, a] = diffs[a] * inv
        gate = (mask[0, 0, k] * tl[0, 0, k, 2]).astype(F32).T * (1.0 / NORM_DIV)
        near = jnp.where(dist < CUTOFF, gate, 0.0)
        phase = dist * (math.pi / CUTOFF)
        ubuf[k] = dist * alpha
        envb[k] = 0.5 * (jnp.cos(phase) + 1.0) * near
        envp[k] = (-0.5 * math.pi / CUTOFF) * jnp.sin(phase) * near

    for copy in x_copies:
        copy.wait_recv()

    def filter_group(k, step, x0):
        first = step * GROUP
        shift = lax.rem(blk - first, blk)
        ur = pltpu.roll(ubuf[k], shift, 1)
        er = pltpu.roll(envb[k], shift, 1)
        pr = pltpu.roll(envp[k], shift, 1)
        msg_rows = []
        for half in range(GROUP // SUB):
            for a in range(SUB):
                lane = half * SUB + a
                t = ur[:, lane:lane + 1] - centers
                e = jnp.exp2(-(t * t))
                es[half, a * blk:(a + 1) * blk, :] = e.astype(BF16)
                ds[half, a * blk:(a + 1) * blk, :] = (t * e).astype(BF16)
            pre = jnp.dot(es[half], wc[...], preferred_element_type=F32) + bias
            th = jnp.tanh(pre)
            hs[half] = (jnp.maximum(pre, 0.0) - 0.5 * jnp.log(1.0 + jnp.abs(th))).astype(BF16)
            ts[half] = ((1.0 + th) * jnp.dot(ds[half], wc[...], preferred_element_type=F32)).astype(BF16)
            filt = jnp.dot(hs[half], fc[...], preferred_element_type=F32)
            dfilt = jnp.dot(ts[half], fc[...], preferred_element_type=F32)
            for a in range(SUB):
                lane = half * SUB + a
                fa = filt[a * blk:(a + 1) * blk, :]
                da = dfilt[a * blk:(a + 1) * blk, :]
                e = er[:, lane:lane + 1]
                p = pr[:, lane:lane + 1]
                gv = fa * e
                msg_rows.append(jnp.sum(gv[:, 0:feat] * x0, axis=0, keepdims=True))
                g1_s[k, first + lane] = gv[:, feat:2 * feat].astype(BF16)
                dg_s[k, first + lane] = (da * (e * half_kappa) + fa * p).astype(BF16)
        msg[0, k, pl.ds(pl.multiple_of(first, GROUP), GROUP), :] = jnp.concatenate(msg_rows, axis=0)

    for k in range(slots):
        x0 = xbuf[0][cols[k]]

        def filter_step(step, carry, k=k, x0=x0):
            filter_group(k, step, x0)
            return carry

        lax.fori_loop(0, blk // GROUP, filter_step, 0)

    def reduce_messages(layer):
        to_sib = send(msg.at[layer], sibmsg.at[layer], me_r, sib)
        own_rows = posblk[...]
        sib_rows = rowpos[sib]
        to_sib.wait_recv()

        def share(zz):
            dest = (zz * 2 + core).astype(F32)
            total = None
            for k in range(slots):
                part = jnp.where(own_rows[3 + k:4 + k, :] == dest, 1.0, 0.0) * msg[layer, k]
                part += jnp.where(sib_rows[3 + k:4 + k, :] == dest, 1.0, 0.0) * sibmsg[layer, k]
                total = part if total is None else total + part
            return total

        copies = []
        for o, zz in enumerate(same_peers):
            sbuf[layer, o] = share(zz)
            copies.append(send(sbuf.at[layer, o], rbuf.at[layer, o], me_r, zz * 2 + core))
        total = share(z)
        for o, copy in enumerate(copies):
            copy.wait_recv()
            total = total + rbuf[layer, o]
        return total

    def gather_cotangents(layer, value):
        gbuf[layer][me_c] = value
        mine = gbuf[layer].at[me_c]
        across = [send(mine, mine, me_r, zz * 2 + core) for zz in same_peers]
        local = [send(mine, mine, me_r, sib)]
        return across, local

    def finish_cotangents(layer, across, local):
        for o, copy in enumerate(across):
            copy.wait_recv()
            source = lax.rem(z + nz - (o + 1), nz) * 2 + core
            block = gbuf[layer].at[source]
            local.append(send(block, block, me_r, sib))
        for copy in local:
            copy.wait_recv()

    message = reduce_messages(0)
    act, sig0 = ssp_parts(dot_nn(message, wu1[0]))
    features = features + dot_nn(act, wu2[0])
    x_copies = gather_features(1, dot_nn(features, w_in[1]))
    for copy in x_copies:
        copy.wait_recv()

    for k in range(slots):
        x1 = xbuf[1][cols[k]]

        def message_step(step, carry, k=k, x1=x1):
            first = step * GROUP
            parts = [
                jnp.sum(g1_s[k, first + a].astype(F32) * x1, axis=0, keepdims=True)
                for a in range(GROUP)
            ]
            msg[1, k, pl.ds(pl.multiple_of(first, GROUP), GROUP), :] = jnp.concatenate(parts, axis=0)
            return carry

        lax.fori_loop(0, blk // GROUP, message_step, 0)

    message = reduce_messages(1)
    act, sig1 = ssp_parts(dot_nn(message, wu1[1]))
    features = features + dot_nn(act, wu2[1])

    act, sig_out = ssp_parts(dot_nn(features, wo1[...]))
    e_out[...] = dot_nt(jnp.broadcast_to(wo2[...], (8, wo2.shape[1])), act)[0:1, :]
    grad_feat = dot_nt(sig_out * wo2[...], wo1[...])

    grad_msg = dot_nt(dot_nt(grad_feat, wu2[1]) * sig1, wu1[1])
    across, local = gather_cotangents(1, grad_msg)
    finish_cotangents(1, across, local)

    for k in range(slots):
        def dx_step(step, acc, k=k):
            first = pl.multiple_of(step * GROUP, GROUP)
            gr = gbuf[1][rows[k], pl.ds(first, GROUP), :]
            for a in range(GROUP):
                acc = acc + g1_s[k, first + a].astype(F32) * gr[a:a + 1, :]
            return acc

        dxs[k] = lax.fori_loop(0, blk // GROUP, dx_step, jnp.zeros((blk, feat), F32))

    own_cols = posblk[...]

    def dx_share(dest):
        total = None
        for k in range(slots):
            part = jnp.where(own_cols[3 + slots + k:4 + slots + k, :] == dest.astype(F32), 1.0, 0.0) * dxs[k]
            total = part if total is None else total + part
        return total

    dx_copies = []
    for o, (r, c) in enumerate(row_peers):
        dxsend[o] = dx_share(r)
        dx_copies.append(send(dxsend.at[o], dxrecv.at[o], r, c))
    grad_in = dx_share(me_r)

    lane_id = lax.broadcasted_iota(jnp.int32, (blk, blk), 1)

    def pair_slopes(layer, k, begin):
        xk = xbuf[layer][cols[k]]

        def slope_step(step, acc):
            first = pl.multiple_of(step * GROUP, GROUP)
            gr = gbuf[layer][rows[k], pl.ds(first, GROUP), :]
            for a in range(GROUP):
                dg = dg_s[k, first + a, :, layer * feat:(layer + 1) * feat].astype(F32)
                red = jnp.sum(dg * (xk * gr[a:a + 1, :]), axis=1, keepdims=True)
                acc = jnp.where(lane_id == first + a, acc + red, acc)
            return acc

        return lax.fori_loop(0, blk // GROUP, slope_step, begin)

    for o, copy in enumerate(dx_copies):
        copy.wait_recv()
        grad_in = grad_in + dxrecv[o]
    grad_feat = grad_feat + dot_nt(grad_in, w_in[1])
    grad_msg = dot_nt(dot_nt(grad_feat, wu2[0]) * sig0, wu1[0])
    across, local = gather_cotangents(0, grad_msg)
    for k in range(slots):
        st[k] = pair_slopes(1, k, jnp.zeros((blk, blk), F32))
    finish_cotangents(0, across, local)

    row_force, col_force = [], []
    for k in range(slots):
        slope = pair_slopes(0, k, st[k])
        rf, cf = [], []
        for a in range(3):
            pull = slope * unit[k, a]
            rf.append(jnp.sum(pull, axis=0, keepdims=True))
            cf.append(-jnp.sum(pull.T, axis=0, keepdims=True))
        pad = jnp.zeros((5, blk), F32)
        row_force.append(jnp.concatenate(rf + [pad], axis=0))
        col_force.append(jnp.concatenate(cf + [pad], axis=0))

    def force_share(parts, base, dest):
        total = None
        for k in range(slots):
            part = jnp.where(own_cols[base + k:base + k + 1, :] == dest.astype(F32), 1.0, 0.0) * parts[k]
            total = part if total is None else total + part
        return total

    copies = []
    for o, (r, c) in enumerate(col_peers):
        rfsend[o] = force_share(row_force, 3, c)
        copies.append((send(rfsend.at[o], rfrecv.at[o], r, c), rfrecv, o))
    for o, (r, c) in enumerate(row_peers):
        cfsend[o] = force_share(col_force, 3 + slots, r)
        copies.append((send(cfsend.at[o], cfrecv.at[o], r, c), cfrecv, o))
    total = force_share(row_force, 3, me_c) + force_share(col_force, 3 + slots, me_r)
    for copy, ref, o in copies:
        copy.wait_recv()
        total = total + ref[o]
    f_out[...] = -total[0:3, :]
    for copy in started:
        copy.wait_send()


def body(n_row, n_col, positions, species, tile_list, pair_mask, embed, w_in, rbf_weight, rbf_bias,
         filt_weight, w_update1, w_update2, w_out1, w_out2):
    blk = positions.shape[1]
    feat = embed.shape[1]
    slots = tile_list.shape[2]
    n_gauss = rbf_weight.shape[1]
    nz = n_col // 2
    n_sems = (
        (n_col - 1 + n_row - 1) * 2 + 2 * (n_row - 1) + 2 * (1 + nz - 1)
        + 2 * (2 * nz - 1) + (n_row - 1)
    )
    vm = pltpu.VMEM
    sub = SUB * blk
    scratch = [
        vm((8, blk), F32), vm((n_col, 8, blk), F32), vm((n_row, 8, blk), F32),
        vm((blk, feat), F32), vm((n_gauss, 2 * feat), BF16), vm((2 * feat, 2 * feat), BF16),
        vm((slots, blk, blk), F32), vm((slots, blk, blk), F32), vm((slots, blk, blk), F32),
        vm((slots, 3, blk, blk), F32),
        vm((GROUP // SUB, sub, n_gauss), BF16), vm((GROUP // SUB, sub, n_gauss), BF16),
        vm((GROUP // SUB, sub, 2 * feat), BF16), vm((GROUP // SUB, sub, 2 * feat), BF16),
        vm((slots, blk, blk, feat), BF16), vm((slots, blk, blk, 2 * feat), BF16),
        vm((2, slots, blk, feat), F32), vm((2, slots, blk, feat), F32),
        vm((2, nz - 1, blk, feat), F32), vm((2, nz - 1, blk, feat), F32),
        vm((n_row, blk, feat), F32), vm((n_row, blk, feat), F32),
        vm((n_col, blk, feat), F32), vm((n_col, blk, feat), F32),
        vm((slots, blk, feat), F32),
        vm((n_row - 1, blk, feat), F32), vm((n_row - 1, blk, feat), F32),
        vm((slots, blk, blk), F32),
        vm((n_col - 1, 8, blk), F32), vm((n_col - 1, 8, blk), F32),
        vm((n_row - 1, 8, blk), F32), vm((n_row - 1, 8, blk), F32),
        pltpu.SemaphoreType.DMA((n_sems,)), pltpu.SemaphoreType.DMA((n_sems,)),
    ]
    vspec = pl.BlockSpec(memory_space=pltpu.VMEM)
    energies, forces = pl.pallas_call(
        partial(kernel, n_row, n_col, slots),
        out_shape=(jax.ShapeDtypeStruct((1, blk), F32), jax.ShapeDtypeStruct((3, blk), F32)),
        in_specs=[pl.BlockSpec(memory_space=pltpu.SMEM)] + [vspec] * 12,
        out_specs=(vspec, vspec),
        scratch_shapes=scratch,
        compiler_params=pltpu.CompilerParams(
            collective_id=0, has_side_effects=True, vmem_limit_bytes=56 * 1024 * 1024),
    )(tile_list, positions, species.reshape(1, blk), pair_mask, embed, w_in, rbf_weight, rbf_bias,
      filt_weight, w_update1, w_update2, w_out1, w_out2.reshape(1, w_out2.shape[0]))
    return energies.reshape(blk), forces


def solution(mesh):
    n_row, n_col = mesh.shape["row"], mesh.shape["col"]
    return jax.shard_map(
        partial(body, n_row, n_col),
        mesh=mesh,
        in_specs=(
            P(None, ("row", "col")),
            P(("row", "col")),
            P("row", "col", None, None),
            P("row", "col", None, None, None),
            P(), P(), P(), P(), P(), P(), P(), P(), P(),
        ),
        out_specs=(P(("row", "col")), P(None, ("row", "col"))),
        check_vma=False,
    )
```

```python
from functools import partial
import math

import jax
import jax.numpy as jnp
from jax import lax
from jax.experimental import pallas as pl
from jax.experimental.pallas import tpu as pltpu
from jax.sharding import PartitionSpec as P

CUTOFF = 5.0
NORM_DIV = 4.0
HIGH = lax.Precision.HIGHEST
MESH = pl.DeviceIdType.MESH
GROUP = 8
SUB = 4
F32 = jnp.float32
BF16 = jnp.bfloat16


def ssp_parts(values):
    th = jnp.tanh(0.5 * values)
    return jnp.maximum(values, 0.0) - jnp.log(1.0 + jnp.abs(th)), 0.5 * (1.0 + th)


def dot_nn(a, b):
    return lax.dot_general(a, b, (((1,), (0,)), ((), ())), precision=HIGH, preferred_element_type=F32)


def dot_nt(a, b):
    return lax.dot_general(a, b, (((1,), (1,)), ((), ())), precision=HIGH, preferred_element_type=F32)


def kernel(
    n_row, n_col, slots,
    tl, pos, spec, mask, embed, w_in, rbf_w, rbf_b, filt_w, wu1, wu2, wo1, wo2,
    e_out, f_out,
    posblk, rowpos, colpos, emb_s, wc, fc,
    ubuf, envb, envp, unit, es, ds, hs, ts,
    g1_s, dg_s, msg, sibmsg, sbuf, rbuf, xbuf0, xbuf1, gbuf0, gbuf1, dxs, dxsend, dxrecv,
    st, rfsend, rfrecv, cfsend, cfrecv,
    send_sem, recv_sem,
):
    blk = pos.shape[1]
    feat = w_in.shape[2]
    n_gauss = rbf_w.shape[1]
    nz = n_col // 2
    me_r = lax.axis_index("row")
    me_c = lax.axis_index("col")
    z = me_c // 2
    core = me_c % 2
    sib = z * 2 + (1 - core)
    started = []
    xbuf, gbuf = (xbuf0, xbuf1), (gbuf0, gbuf1)

    def send(src, dst, r, c):
        n = len(started)
        copy = pltpu.make_async_remote_copy(
            src_ref=src, dst_ref=dst, send_sem=send_sem.at[n], recv_sem=recv_sem.at[n],
            device_id=(r, c), device_id_type=MESH)
        copy.start()
        started.append(copy)
        return copy

    row_peers = [(lax.rem(me_r + o, n_row), me_c) for o in range(1, n_row)]
    col_peers = [(me_r, lax.rem(me_c + o, n_col)) for o in range(1, n_col)]
    same_peers = [lax.rem(z + o, nz) for o in range(1, nz)]

    barrier = pltpu.get_barrier_semaphore()
    for peer in row_peers + col_peers:
        pl.semaphore_signal(barrier, inc=1, device_id=peer, device_id_type=MESH)

    posblk[...] = jnp.zeros_like(posblk)
    posblk[0:3, :] = pos[...]
    for k in range(slots):
        posblk[3 + k:4 + k, :] = jnp.full((1, blk), tl[0, 0, k, 0], jnp.int32).astype(F32)
        posblk[3 + slots + k:4 + slots + k, :] = jnp.full((1, blk), tl[0, 0, k, 1], jnp.int32).astype(F32)
    rowpos[me_c] = posblk[...]
    colpos[me_r] = posblk[...]

    pl.semaphore_wait(barrier, len(row_peers) + len(col_peers))
    pos_copies = [send(posblk, rowpos.at[me_c], *peer) for peer in col_peers]
    pos_copies += [send(posblk, colpos.at[me_r], *peer) for peer in row_peers]

    emb_s[...] = jnp.zeros_like(emb_s)
    emb_s[0:embed.shape[0], :] = embed[...]
    onehot_t = (lax.broadcasted_iota(jnp.int32, (blk, blk), 0) == spec[...]).astype(F32)
    features = dot_nn(onehot_t.T, emb_s[...])

    def gather_features(layer, value):
        xbuf[layer][me_r] = value
        return [send(xbuf[layer].at[me_r], xbuf[layer].at[me_r], *peer) for peer in row_peers]

    x_copies = gather_features(0, dot_nn(features, w_in[0]))

    wc[:, 0:feat] = (rbf_w[0].astype(F32) * 0.5).astype(BF16)
    wc[:, feat:2 * feat] = (rbf_w[1].astype(F32) * 0.5).astype(BF16)
    fc[...] = jnp.zeros_like(fc)
    fc[0:feat, 0:feat] = (filt_w[0].astype(F32) * 2.0).astype(BF16)
    fc[feat:2 * feat, feat:2 * feat] = (filt_w[1].astype(F32) * 2.0).astype(BF16)
    bias = 0.5 * jnp.concatenate([rbf_b[0:1, :], rbf_b[1:2, :]], axis=1)

    sharp = (n_gauss / CUTOFF) ** 2 / 32.0
    alpha = math.sqrt(sharp / math.log(2.0))
    centers = lax.broadcasted_iota(jnp.int32, (1, n_gauss), 1).astype(F32) * (alpha * CUTOFF / n_gauss)
    half_kappa = -math.log(2.0) * alpha

    for copy in pos_copies:
        copy.wait_recv()

    rows = [tl[0, 0, k, 0] for k in range(slots)]
    cols = [tl[0, 0, k, 1] for k in range(slots)]
    for k in range(slots):
        rp = rowpos[rows[k]]
        cp = colpos[cols[k]]
        diffs = []
        for a in range(3):
            pj = jnp.broadcast_to(cp[a:a + 1, :], (blk, blk)).T
            diffs.append(rp[a:a + 1, :] - pj)
        dist = jnp.sqrt(diffs[0] * diffs[0] + diffs[1] * diffs[1] + diffs[2] * diffs[2] + 0.01)
        inv = 1.0 / dist
        for a in range(3):
            unit[k, a] = diffs[a] * inv
        gate = (mask[0, 0, k] * tl[0, 0, k, 2]).astype(F32).T * (1.0 / NORM_DIV)
        near = jnp.where(dist < CUTOFF, gate, 0.0)
        phase = dist * (math.pi / CUTOFF)
        ubuf[k] = dist * alpha
        envb[k] = 0.5 * (jnp.cos(phase) + 1.0) * near
        envp[k] = (-0.5 * math.pi / CUTOFF) * jnp.sin(phase) * near

    for copy in x_copies:
        copy.wait_recv()

    def filter_group(k, step, x0, forward, slope):
        first = step * GROUP
        shift = lax.rem(blk - first, blk)
        ur = pltpu.roll(ubuf[k], shift, 1)
        er = pltpu.roll(envb[k], shift, 1)
        pr = pltpu.roll(envp[k], shift, 1) if slope else None
        msg_rows = []
        for half in range(GROUP // SUB):
            for a in range(SUB):
                lane = half * SUB + a
                t = ur[:, lane:lane + 1] - centers
                e = jnp.exp2(-(t * t))
                es[half, a * blk:(a + 1) * blk, :] = e.astype(BF16)
                if slope:
                    ds[half, a * blk:(a + 1) * blk, :] = (t * e).astype(BF16)
            pre = jnp.dot(es[half], wc[...], preferred_element_type=F32) + bias
            th = jnp.tanh(pre)
            hs[half] = (jnp.maximum(pre, 0.0) - 0.5 * jnp.log(1.0 + jnp.abs(th))).astype(BF16)
            filt = jnp.dot(hs[half], fc[...], preferred_element_type=F32)
            if slope:
                ts[half] = ((1.0 + th) * jnp.dot(ds[half], wc[...], preferred_element_type=F32)).astype(BF16)
                dfilt = jnp.dot(ts[half], fc[...], preferred_element_type=F32)
            for a in range(SUB):
                lane = half * SUB + a
                fa = filt[a * blk:(a + 1) * blk, :]
                e = er[:, lane:lane + 1]
                if forward:
                    gv = fa * e
                    msg_rows.append(jnp.sum(gv[:, 0:feat] * x0, axis=0, keepdims=True))
                    g1_s[k, first + lane] = gv[:, feat:2 * feat].astype(BF16)
                if slope:
                    da = dfilt[a * blk:(a + 1) * blk, :]
                    p = pr[:, lane:lane + 1]
                    dg_s[k, first + lane] = (da * (e * half_kappa) + fa * p).astype(BF16)
        if forward:
            msg[0, k, pl.ds(pl.multiple_of(first, GROUP), GROUP), :] = jnp.concatenate(msg_rows, axis=0)

    steps = blk // GROUP
    late = slots - 1
    parts = 4
    cuts = [steps * p // parts for p in range(parts + 1)]

    def late_slopes(part):
        def late_step(step, carry):
            filter_group(late, step, None, False, True)
            return carry

        lax.fori_loop(cuts[part], cuts[part + 1], late_step, 0)

    to_sib = [[], []]

    def send_message(layer, k):
        to_sib[layer].append(send(msg.at[layer, k], sibmsg.at[layer, k], me_r, sib))

    for k in range(slots):
        x0 = xbuf[0][cols[k]]

        def filter_step(step, carry, k=k, x0=x0):
            filter_group(k, step, x0, True, k != late)
            return carry

        lax.fori_loop(0, steps, filter_step, 0)
        send_message(0, k)

    def reduce_messages(layer, part):
        own_rows = posblk[...]
        sib_rows = rowpos[sib]
        for copy in to_sib[layer]:
            copy.wait_recv()

        def share(zz):
            dest = (zz * 2 + core).astype(F32)
            total = None
            for k in range(slots):
                part = jnp.where(own_rows[3 + k:4 + k, :] == dest, 1.0, 0.0) * msg[layer, k]
                part += jnp.where(sib_rows[3 + k:4 + k, :] == dest, 1.0, 0.0) * sibmsg[layer, k]
                total = part if total is None else total + part
            return total

        copies = []
        for o, zz in enumerate(same_peers):
            sbuf[layer, o] = share(zz)
            copies.append(send(sbuf.at[layer, o], rbuf.at[layer, o], me_r, zz * 2 + core))
        total = share(z)
        late_slopes(part)
        for o, copy in enumerate(copies):
            copy.wait_recv()
            total = total + rbuf[layer, o]
        return total

    def gather_cotangents(layer, value):
        gbuf[layer][me_c] = value
        mine = gbuf[layer].at[me_c]
        across = [send(mine, mine, me_r, zz * 2 + core) for zz in same_peers]
        local = [send(mine, mine, me_r, sib)]
        return across, local

    def finish_cotangents(layer, across, local):
        for o, copy in enumerate(across):
            copy.wait_recv()
            source = lax.rem(z + nz - (o + 1), nz) * 2 + core
            block = gbuf[layer].at[source]
            local.append(send(block, block, me_r, sib))
        for copy in local:
            copy.wait_recv()

    message = reduce_messages(0, 0)
    act, sig0 = ssp_parts(dot_nn(message, wu1[0]))
    features = features + dot_nn(act, wu2[0])
    x_copies = gather_features(1, dot_nn(features, w_in[1]))
    late_slopes(1)
    for copy in x_copies:
        copy.wait_recv()

    for k in range(slots):
        x1 = xbuf[1][cols[k]]

        def message_step(step, carry, k=k, x1=x1):
            first = step * GROUP
            lines = [
                jnp.sum(g1_s[k, first + a].astype(F32) * x1, axis=0, keepdims=True)
                for a in range(GROUP)
            ]
            msg[1, k, pl.ds(pl.multiple_of(first, GROUP), GROUP), :] = jnp.concatenate(lines, axis=0)
            return carry

        lax.fori_loop(0, steps, message_step, 0)
        send_message(1, k)

    message = reduce_messages(1, 2)
    act, sig1 = ssp_parts(dot_nn(message, wu1[1]))
    features = features + dot_nn(act, wu2[1])

    act, sig_out = ssp_parts(dot_nn(features, wo1[...]))
    e_out[...] = dot_nt(jnp.broadcast_to(wo2[...], (8, wo2.shape[1])), act)[0:1, :]
    grad_feat = dot_nt(sig_out * wo2[...], wo1[...])

    grad_msg = dot_nt(dot_nt(grad_feat, wu2[1]) * sig1, wu1[1])
    across, local = gather_cotangents(1, grad_msg)
    late_slopes(3)
    finish_cotangents(1, across, local)

    for k in range(slots):
        def dx_step(step, acc, k=k):
            first = pl.multiple_of(step * GROUP, GROUP)
            gr = gbuf[1][rows[k], pl.ds(first, GROUP), :]
            for a in range(GROUP):
                acc = acc + g1_s[k, first + a].astype(F32) * gr[a:a + 1, :]
            return acc

        dxs[k] = lax.fori_loop(0, blk // GROUP, dx_step, jnp.zeros((blk, feat), F32))

    own_cols = posblk[...]

    def dx_share(dest):
        total = None
        for k in range(slots):
            part = jnp.where(own_cols[3 + slots + k:4 + slots + k, :] == dest.astype(F32), 1.0, 0.0) * dxs[k]
            total = part if total is None else total + part
        return total

    dx_copies = []
    for o, (r, c) in enumerate(row_peers):
        dxsend[o] = dx_share(r)
        dx_copies.append(send(dxsend.at[o], dxrecv.at[o], r, c))
    grad_in = dx_share(me_r)

    lane_id = lax.broadcasted_iota(jnp.int32, (blk, blk), 1)

    def pair_slopes(layer, k, begin):
        xk = xbuf[layer][cols[k]]

        def slope_step(step, acc):
            first = pl.multiple_of(step * GROUP, GROUP)
            gr = gbuf[layer][rows[k], pl.ds(first, GROUP), :]
            for a in range(GROUP):
                dg = dg_s[k, first + a, :, layer * feat:(layer + 1) * feat].astype(F32)
                red = jnp.sum(dg * (xk * gr[a:a + 1, :]), axis=1, keepdims=True)
                acc = jnp.where(lane_id == first + a, acc + red, acc)
            return acc

        return lax.fori_loop(0, blk // GROUP, slope_step, begin)

    for o, copy in enumerate(dx_copies):
        copy.wait_recv()
        grad_in = grad_in + dxrecv[o]
    grad_feat = grad_feat + dot_nt(grad_in, w_in[1])
    grad_msg = dot_nt(dot_nt(grad_feat, wu2[0]) * sig0, wu1[0])
    across, local = gather_cotangents(0, grad_msg)
    for k in range(slots):
        st[k] = pair_slopes(1, k, jnp.zeros((blk, blk), F32))
    finish_cotangents(0, across, local)

    row_force, col_force = [], []
    for k in range(slots):
        slope = pair_slopes(0, k, st[k])
        rf, cf = [], []
        for a in range(3):
            pull = slope * unit[k, a]
            rf.append(jnp.sum(pull, axis=0, keepdims=True))
            cf.append(-jnp.sum(pull.T, axis=0, keepdims=True))
        pad = jnp.zeros((5, blk), F32)
        row_force.append(jnp.concatenate(rf + [pad], axis=0))
        col_force.append(jnp.concatenate(cf + [pad], axis=0))

    def force_share(parts, base, dest):
        total = None
        for k in range(slots):
            part = jnp.where(own_cols[base + k:base + k + 1, :] == dest.astype(F32), 1.0, 0.0) * parts[k]
            total = part if total is None else total + part
        return total

    copies = []
    for o, (r, c) in enumerate(col_peers):
        rfsend[o] = force_share(row_force, 3, c)
        copies.append((send(rfsend.at[o], rfrecv.at[o], r, c), rfrecv, o))
    for o, (r, c) in enumerate(row_peers):
        cfsend[o] = force_share(col_force, 3 + slots, r)
        copies.append((send(cfsend.at[o], cfrecv.at[o], r, c), cfrecv, o))
    total = force_share(row_force, 3, me_c) + force_share(col_force, 3 + slots, me_r)
    for copy, ref, o in copies:
        copy.wait_recv()
        total = total + ref[o]
    f_out[...] = -total[0:3, :]
    for copy in started:
        copy.wait_send()


def body(n_row, n_col, positions, species, tile_list, pair_mask, embed, w_in, rbf_weight, rbf_bias,
         filt_weight, w_update1, w_update2, w_out1, w_out2):
    blk = positions.shape[1]
    feat = embed.shape[1]
    slots = tile_list.shape[2]
    n_gauss = rbf_weight.shape[1]
    nz = n_col // 2
    n_sems = (
        (n_col - 1 + n_row - 1) * 2 + 2 * (n_row - 1) + 2 * (slots + nz - 1)
        + 2 * (2 * nz - 1) + (n_row - 1)
    )
    vm = pltpu.VMEM
    sub = SUB * blk
    scratch = [
        vm((8, blk), F32), vm((n_col, 8, blk), F32), vm((n_row, 8, blk), F32),
        vm((blk, feat), F32), vm((n_gauss, 2 * feat), BF16), vm((2 * feat, 2 * feat), BF16),
        vm((slots, blk, blk), F32), vm((slots, blk, blk), F32), vm((slots, blk, blk), F32),
        vm((slots, 3, blk, blk), F32),
        vm((GROUP // SUB, sub, n_gauss), BF16), vm((GROUP // SUB, sub, n_gauss), BF16),
        vm((GROUP // SUB, sub, 2 * feat), BF16), vm((GROUP // SUB, sub, 2 * feat), BF16),
        vm((slots, blk, blk, feat), BF16), vm((slots, blk, blk, 2 * feat), BF16),
        vm((2, slots, blk, feat), F32), vm((2, slots, blk, feat), F32),
        vm((2, nz - 1, blk, feat), F32), vm((2, nz - 1, blk, feat), F32),
        vm((n_row, blk, feat), F32), vm((n_row, blk, feat), F32),
        vm((n_col, blk, feat), F32), vm((n_col, blk, feat), F32),
        vm((slots, blk, feat), F32),
        vm((n_row - 1, blk, feat), F32), vm((n_row - 1, blk, feat), F32),
        vm((slots, blk, blk), F32),
        vm((n_col - 1, 8, blk), F32), vm((n_col - 1, 8, blk), F32),
        vm((n_row - 1, 8, blk), F32), vm((n_row - 1, 8, blk), F32),
        pltpu.SemaphoreType.DMA((n_sems,)), pltpu.SemaphoreType.DMA((n_sems,)),
    ]
    vspec = pl.BlockSpec(memory_space=pltpu.VMEM)
    energies, forces = pl.pallas_call(
        partial(kernel, n_row, n_col, slots),
        out_shape=(jax.ShapeDtypeStruct((1, blk), F32), jax.ShapeDtypeStruct((3, blk), F32)),
        in_specs=[pl.BlockSpec(memory_space=pltpu.SMEM)] + [vspec] * 12,
        out_specs=(vspec, vspec),
        scratch_shapes=scratch,
        compiler_params=pltpu.CompilerParams(
            collective_id=0, has_side_effects=True, vmem_limit_bytes=56 * 1024 * 1024),
    )(tile_list, positions, species.reshape(1, blk), pair_mask, embed, w_in, rbf_weight, rbf_bias,
      filt_weight, w_update1, w_update2, w_out1, w_out2.reshape(1, w_out2.shape[0]))
    return energies.reshape(blk), forces


def solution(mesh):
    n_row, n_col = mesh.shape["row"], mesh.shape["col"]
    return jax.shard_map(
        partial(body, n_row, n_col),
        mesh=mesh,
        in_specs=(
            P(None, ("row", "col")),
            P(("row", "col")),
            P("row", "col", None, None),
            P("row", "col", None, None, None),
            P(), P(), P(), P(), P(), P(), P(), P(), P(),
        ),
        out_specs=(P(("row", "col")), P(None, ("row", "col"))),
        check_vma=False,
    )
```

```python
from functools import partial
import math

import jax
import jax.numpy as jnp
from jax import lax
from jax.experimental import pallas as pl
from jax.experimental.pallas import tpu as pltpu
from jax.sharding import PartitionSpec as P

CUTOFF = 5.0
NORM_DIV = 4.0
HIGH = lax.Precision.HIGHEST
MESH = pl.DeviceIdType.MESH
GROUP = 16
SUB = 4
F32 = jnp.float32
BF16 = jnp.bfloat16


def ssp_parts(values):
    th = jnp.tanh(0.5 * values)
    return jnp.maximum(values, 0.0) - jnp.log(1.0 + jnp.abs(th)), 0.5 * (1.0 + th)


def dot_nn(a, b):
    return lax.dot_general(a, b, (((1,), (0,)), ((), ())), precision=HIGH, preferred_element_type=F32)


def dot_nt(a, b):
    return lax.dot_general(a, b, (((1,), (1,)), ((), ())), precision=HIGH, preferred_element_type=F32)


def kernel(
    n_row, n_col, slots,
    tl, pos, spec, mask, embed, w_in, rbf_w, rbf_b, filt_w, wu1, wu2, wo1, wo2,
    e_out, f_out,
    posblk, rowpos, colpos, emb_s, wc, fc,
    ubuf, envb, envp, unit, es, ds, hs, ts,
    g1_s, dg_s, msg, sibmsg, sbuf, rbuf, xbuf0, xbuf1, gbuf0, gbuf1, dxs, dxsend, dxrecv,
    st, rfsend, rfrecv, cfsend, cfrecv,
    send_sem, recv_sem,
):
    blk = pos.shape[1]
    feat = w_in.shape[2]
    n_gauss = rbf_w.shape[1]
    nz = n_col // 2
    me_r = lax.axis_index("row")
    me_c = lax.axis_index("col")
    z = me_c // 2
    core = me_c % 2
    sib = z * 2 + (1 - core)
    started = []
    xbuf, gbuf = (xbuf0, xbuf1), (gbuf0, gbuf1)

    def send(src, dst, r, c):
        n = len(started)
        copy = pltpu.make_async_remote_copy(
            src_ref=src, dst_ref=dst, send_sem=send_sem.at[n], recv_sem=recv_sem.at[n],
            device_id=(r, c), device_id_type=MESH)
        copy.start()
        started.append(copy)
        return copy

    row_peers = [(lax.rem(me_r + o, n_row), me_c) for o in range(1, n_row)]
    col_peers = [(me_r, lax.rem(me_c + o, n_col)) for o in range(1, n_col)]
    same_peers = [lax.rem(z + o, nz) for o in range(1, nz)]

    barrier = pltpu.get_barrier_semaphore()
    for peer in row_peers + col_peers:
        pl.semaphore_signal(barrier, inc=1, device_id=peer, device_id_type=MESH)

    posblk[...] = jnp.zeros_like(posblk)
    posblk[0:3, :] = pos[...]
    for k in range(slots):
        posblk[3 + k:4 + k, :] = jnp.full((1, blk), tl[0, 0, k, 0], jnp.int32).astype(F32)
        posblk[3 + slots + k:4 + slots + k, :] = jnp.full((1, blk), tl[0, 0, k, 1], jnp.int32).astype(F32)
    rowpos[me_c] = posblk[...]
    colpos[me_r] = posblk[...]

    pl.semaphore_wait(barrier, len(row_peers) + len(col_peers))
    pos_copies = [send(posblk, rowpos.at[me_c], *peer) for peer in col_peers]
    pos_copies += [send(posblk, colpos.at[me_r], *peer) for peer in row_peers]

    emb_s[...] = jnp.zeros_like(emb_s)
    emb_s[0:embed.shape[0], :] = embed[...]
    onehot_t = (lax.broadcasted_iota(jnp.int32, (blk, blk), 0) == spec[...]).astype(F32)
    features = dot_nn(onehot_t.T, emb_s[...])

    def gather_features(layer, value):
        xbuf[layer][me_r] = value
        return [send(xbuf[layer].at[me_r], xbuf[layer].at[me_r], *peer) for peer in row_peers]

    x_copies = gather_features(0, dot_nn(features, w_in[0]))

    wc[:, 0:feat] = (rbf_w[0].astype(F32) * 0.5).astype(BF16)
    wc[:, feat:2 * feat] = (rbf_w[1].astype(F32) * 0.5).astype(BF16)
    fc[...] = jnp.zeros_like(fc)
    fc[0:feat, 0:feat] = (filt_w[0].astype(F32) * 2.0).astype(BF16)
    fc[feat:2 * feat, feat:2 * feat] = (filt_w[1].astype(F32) * 2.0).astype(BF16)
    bias = 0.5 * jnp.concatenate([rbf_b[0:1, :], rbf_b[1:2, :]], axis=1)

    sharp = (n_gauss / CUTOFF) ** 2 / 32.0
    alpha = math.sqrt(sharp)
    centers = lax.broadcasted_iota(jnp.int32, (1, n_gauss), 1).astype(F32) * (alpha * CUTOFF / n_gauss)
    half_kappa = -alpha

    for copy in pos_copies:
        copy.wait_recv()

    rows = [tl[0, 0, k, 0] for k in range(slots)]
    cols = [tl[0, 0, k, 1] for k in range(slots)]
    for k in range(slots):
        rp = rowpos[rows[k]]
        cp = colpos[cols[k]]
        diffs = []
        for a in range(3):
            pj = jnp.broadcast_to(cp[a:a + 1, :], (blk, blk)).T
            diffs.append(rp[a:a + 1, :] - pj)
        dist = jnp.sqrt(diffs[0] * diffs[0] + diffs[1] * diffs[1] + diffs[2] * diffs[2] + 0.01)
        inv = 1.0 / dist
        for a in range(3):
            unit[k, a] = diffs[a] * inv
        gate = (mask[0, 0, k] * tl[0, 0, k, 2]).astype(F32).T * (1.0 / NORM_DIV)
        near = jnp.where(dist < CUTOFF, gate, 0.0)
        phase = dist * (math.pi / CUTOFF)
        ubuf[k] = dist * alpha
        envb[k] = 0.5 * (jnp.cos(phase) + 1.0) * near
        envp[k] = (-0.5 * math.pi / CUTOFF) * jnp.sin(phase) * near

    for copy in x_copies:
        copy.wait_recv()

    def filter_group(k, step, x0, forward, slope):
        first = step * GROUP
        shift = lax.rem(blk - first, blk)
        ur = pltpu.roll(ubuf[k], shift, 1)
        er = pltpu.roll(envb[k], shift, 1)
        pr = pltpu.roll(envp[k], shift, 1) if slope else None
        msg_rows = []
        for half in range(GROUP // SUB):
            for a in range(SUB):
                lane = half * SUB + a
                t = ur[:, lane:lane + 1] - centers
                e = jnp.exp(-(t * t))
                es[half, a * blk:(a + 1) * blk, :] = e.astype(BF16)
                if slope:
                    ds[half, a * blk:(a + 1) * blk, :] = (t * e).astype(BF16)
            pre = jnp.dot(es[half], wc[...], preferred_element_type=F32) + bias
            th = jnp.tanh(pre)
            hs[half] = (jnp.maximum(pre, 0.0) - 0.5 * jnp.log(1.0 + jnp.abs(th))).astype(BF16)
            filt = jnp.dot(hs[half], fc[...], preferred_element_type=F32)
            if slope:
                ts[half] = ((1.0 + th) * jnp.dot(ds[half], wc[...], preferred_element_type=F32)).astype(BF16)
                dfilt = jnp.dot(ts[half], fc[...], preferred_element_type=F32)
            for a in range(SUB):
                lane = half * SUB + a
                fa = filt[a * blk:(a + 1) * blk, :]
                e = er[:, lane:lane + 1]
                if forward:
                    gv = fa * e
                    msg_rows.append(jnp.sum(gv[:, 0:feat] * x0, axis=0, keepdims=True))
                    g1_s[k, first + lane] = gv[:, feat:2 * feat].astype(BF16)
                if slope:
                    da = dfilt[a * blk:(a + 1) * blk, :]
                    p = pr[:, lane:lane + 1]
                    dg_s[k, first + lane] = (da * (e * half_kappa) + fa * p).astype(BF16)
        if forward:
            msg[0, k, pl.ds(pl.multiple_of(first, GROUP), GROUP), :] = jnp.concatenate(msg_rows, axis=0)

    steps = blk // GROUP
    late = slots - 1
    parts = 4
    cuts = [steps * p // parts for p in range(parts + 1)]

    def late_slopes(part):
        def late_step(step, carry):
            filter_group(late, step, None, False, True)
            return carry

        lax.fori_loop(cuts[part], cuts[part + 1], late_step, 0)

    to_sib = [[], []]

    def send_message(layer, k):
        to_sib[layer].append(send(msg.at[layer, k], sibmsg.at[layer, k], me_r, sib))

    for k in range(slots):
        x0 = xbuf[0][cols[k]]

        def filter_step(step, carry, k=k, x0=x0):
            filter_group(k, step, x0, True, k != late)
            return carry

        lax.fori_loop(0, steps, filter_step, 0)
        send_message(0, k)

    def reduce_messages(layer, part):
        own_rows = posblk[...]
        sib_rows = rowpos[sib]
        for copy in to_sib[layer]:
            copy.wait_recv()

        def share(zz):
            dest = (zz * 2 + core).astype(F32)
            total = None
            for k in range(slots):
                part = jnp.where(own_rows[3 + k:4 + k, :] == dest, 1.0, 0.0) * msg[layer, k]
                part += jnp.where(sib_rows[3 + k:4 + k, :] == dest, 1.0, 0.0) * sibmsg[layer, k]
                total = part if total is None else total + part
            return total

        copies = []
        for o, zz in enumerate(same_peers):
            sbuf[layer, o] = share(zz)
            copies.append(send(sbuf.at[layer, o], rbuf.at[layer, o], me_r, zz * 2 + core))
        total = share(z)
        late_slopes(part)
        for o, copy in enumerate(copies):
            copy.wait_recv()
            total = total + rbuf[layer, o]
        return total

    def gather_cotangents(layer, value):
        gbuf[layer][me_c] = value
        mine = gbuf[layer].at[me_c]
        across = [send(mine, mine, me_r, zz * 2 + core) for zz in same_peers]
        local = [send(mine, mine, me_r, sib)]
        return across, local

    def finish_cotangents(layer, across, local):
        for o, copy in enumerate(across):
            copy.wait_recv()
            source = lax.rem(z + nz - (o + 1), nz) * 2 + core
            block = gbuf[layer].at[source]
            local.append(send(block, block, me_r, sib))
        for copy in local:
            copy.wait_recv()

    message = reduce_messages(0, 0)
    act, sig0 = ssp_parts(dot_nn(message, wu1[0]))
    features = features + dot_nn(act, wu2[0])
    x_copies = gather_features(1, dot_nn(features, w_in[1]))
    late_slopes(1)
    for copy in x_copies:
        copy.wait_recv()

    for k in range(slots):
        x1 = xbuf[1][cols[k]]

        def message_step(step, carry, k=k, x1=x1):
            first = step * GROUP
            lines = [
                jnp.sum(g1_s[k, first + a].astype(F32) * x1, axis=0, keepdims=True)
                for a in range(GROUP)
            ]
            msg[1, k, pl.ds(pl.multiple_of(first, GROUP), GROUP), :] = jnp.concatenate(lines, axis=0)
            return carry

        lax.fori_loop(0, steps, message_step, 0)
        send_message(1, k)

    message = reduce_messages(1, 2)
    act, sig1 = ssp_parts(dot_nn(message, wu1[1]))
    features = features + dot_nn(act, wu2[1])

    act, sig_out = ssp_parts(dot_nn(features, wo1[...]))
    e_out[...] = dot_nt(jnp.broadcast_to(wo2[...], (8, wo2.shape[1])), act)[0:1, :]
    grad_feat = dot_nt(sig_out * wo2[...], wo1[...])

    grad_msg = dot_nt(dot_nt(grad_feat, wu2[1]) * sig1, wu1[1])
    across, local = gather_cotangents(1, grad_msg)
    late_slopes(3)
    finish_cotangents(1, across, local)

    for k in range(slots):
        def dx_step(step, acc, k=k):
            first = pl.multiple_of(step * GROUP, GROUP)
            gr = gbuf[1][rows[k], pl.ds(first, GROUP), :]
            for a in range(GROUP):
                acc = acc + g1_s[k, first + a].astype(F32) * gr[a:a + 1, :]
            return acc

        dxs[k] = lax.fori_loop(0, blk // GROUP, dx_step, jnp.zeros((blk, feat), F32))

    own_cols = posblk[...]

    def dx_share(dest):
        total = None
        for k in range(slots):
            part = jnp.where(own_cols[3 + slots + k:4 + slots + k, :] == dest.astype(F32), 1.0, 0.0) * dxs[k]
            total = part if total is None else total + part
        return total

    dx_copies = []
    for o, (r, c) in enumerate(row_peers):
        dxsend[o] = dx_share(r)
        dx_copies.append(send(dxsend.at[o], dxrecv.at[o], r, c))
    grad_in = dx_share(me_r)

    lane_id = lax.broadcasted_iota(jnp.int32, (blk, blk), 1)

    def pair_slopes(layer, k, begin):
        xk = xbuf[layer][cols[k]]

        def slope_step(step, acc):
            first = pl.multiple_of(step * GROUP, GROUP)
            gr = gbuf[layer][rows[k], pl.ds(first, GROUP), :]
            for a in range(GROUP):
                dg = dg_s[k, first + a, :, layer * feat:(layer + 1) * feat].astype(F32)
                red = jnp.sum(dg * (xk * gr[a:a + 1, :]), axis=1, keepdims=True)
                acc = jnp.where(lane_id == first + a, acc + red, acc)
            return acc

        return lax.fori_loop(0, blk // GROUP, slope_step, begin)

    for o, copy in enumerate(dx_copies):
        copy.wait_recv()
        grad_in = grad_in + dxrecv[o]
    grad_feat = grad_feat + dot_nt(grad_in, w_in[1])
    grad_msg = dot_nt(dot_nt(grad_feat, wu2[0]) * sig0, wu1[0])
    across, local = gather_cotangents(0, grad_msg)
    for k in range(slots):
        st[k] = pair_slopes(1, k, jnp.zeros((blk, blk), F32))
    finish_cotangents(0, across, local)

    row_force, col_force = [], []
    for k in range(slots):
        slope = pair_slopes(0, k, st[k])
        rf, cf = [], []
        for a in range(3):
            pull = slope * unit[k, a]
            rf.append(jnp.sum(pull, axis=0, keepdims=True))
            cf.append(-jnp.sum(pull.T, axis=0, keepdims=True))
        pad = jnp.zeros((5, blk), F32)
        row_force.append(jnp.concatenate(rf + [pad], axis=0))
        col_force.append(jnp.concatenate(cf + [pad], axis=0))

    def force_share(parts, base, dest):
        total = None
        for k in range(slots):
            part = jnp.where(own_cols[base + k:base + k + 1, :] == dest.astype(F32), 1.0, 0.0) * parts[k]
            total = part if total is None else total + part
        return total

    copies = []
    for o, (r, c) in enumerate(col_peers):
        rfsend[o] = force_share(row_force, 3, c)
        copies.append((send(rfsend.at[o], rfrecv.at[o], r, c), rfrecv, o))
    for o, (r, c) in enumerate(row_peers):
        cfsend[o] = force_share(col_force, 3 + slots, r)
        copies.append((send(cfsend.at[o], cfrecv.at[o], r, c), cfrecv, o))
    total = force_share(row_force, 3, me_c) + force_share(col_force, 3 + slots, me_r)
    for copy, ref, o in copies:
        copy.wait_recv()
        total = total + ref[o]
    f_out[...] = -total[0:3, :]
    for copy in started:
        copy.wait_send()


def body(n_row, n_col, positions, species, tile_list, pair_mask, embed, w_in, rbf_weight, rbf_bias,
         filt_weight, w_update1, w_update2, w_out1, w_out2):
    blk = positions.shape[1]
    feat = embed.shape[1]
    slots = tile_list.shape[2]
    n_gauss = rbf_weight.shape[1]
    nz = n_col // 2
    n_sems = (
        (n_col - 1 + n_row - 1) * 2 + 2 * (n_row - 1) + 2 * (slots + nz - 1)
        + 2 * (2 * nz - 1) + (n_row - 1)
    )
    vm = pltpu.VMEM
    sub = SUB * blk
    scratch = [
        vm((8, blk), F32), vm((n_col, 8, blk), F32), vm((n_row, 8, blk), F32),
        vm((blk, feat), F32), vm((n_gauss, 2 * feat), BF16), vm((2 * feat, 2 * feat), BF16),
        vm((slots, blk, blk), F32), vm((slots, blk, blk), F32), vm((slots, blk, blk), F32),
        vm((slots, 3, blk, blk), F32),
        vm((GROUP // SUB, sub, n_gauss), BF16), vm((GROUP // SUB, sub, n_gauss), BF16),
        vm((GROUP // SUB, sub, 2 * feat), BF16), vm((GROUP // SUB, sub, 2 * feat), BF16),
        vm((slots, blk, blk, feat), BF16), vm((slots, blk, blk, 2 * feat), BF16),
        vm((2, slots, blk, feat), F32), vm((2, slots, blk, feat), F32),
        vm((2, nz - 1, blk, feat), F32), vm((2, nz - 1, blk, feat), F32),
        vm((n_row, blk, feat), F32), vm((n_row, blk, feat), F32),
        vm((n_col, blk, feat), F32), vm((n_col, blk, feat), F32),
        vm((slots, blk, feat), F32),
        vm((n_row - 1, blk, feat), F32), vm((n_row - 1, blk, feat), F32),
        vm((slots, blk, blk), F32),
        vm((n_col - 1, 8, blk), F32), vm((n_col - 1, 8, blk), F32),
        vm((n_row - 1, 8, blk), F32), vm((n_row - 1, 8, blk), F32),
        pltpu.SemaphoreType.DMA((n_sems,)), pltpu.SemaphoreType.DMA((n_sems,)),
    ]
    vspec = pl.BlockSpec(memory_space=pltpu.VMEM)
    energies, forces = pl.pallas_call(
        partial(kernel, n_row, n_col, slots),
        out_shape=(jax.ShapeDtypeStruct((1, blk), F32), jax.ShapeDtypeStruct((3, blk), F32)),
        in_specs=[pl.BlockSpec(memory_space=pltpu.SMEM)] + [vspec] * 12,
        out_specs=(vspec, vspec),
        scratch_shapes=scratch,
        compiler_params=pltpu.CompilerParams(
            collective_id=0, has_side_effects=True, vmem_limit_bytes=56 * 1024 * 1024),
    )(tile_list, positions, species.reshape(1, blk), pair_mask, embed, w_in, rbf_weight, rbf_bias,
      filt_weight, w_update1, w_update2, w_out1, w_out2.reshape(1, w_out2.shape[0]))
    return energies.reshape(blk), forces


def solution(mesh):
    n_row, n_col = mesh.shape["row"], mesh.shape["col"]
    return jax.shard_map(
        partial(body, n_row, n_col),
        mesh=mesh,
        in_specs=(
            P(None, ("row", "col")),
            P(("row", "col")),
            P("row", "col", None, None),
            P("row", "col", None, None, None),
            P(), P(), P(), P(), P(), P(), P(), P(), P(),
        ),
        out_specs=(P(("row", "col")), P(None, ("row", "col"))),
        check_vma=False,
    )
```
